128 devices in a mesh: dp: 128 (over z, x, y, core).
Axes of the slice: x: 4, y: 4, z: 4, core: 2. Of those that a mesh axis runs over, the one named last changes fastest.
Arguments:
- image_embed: bfloat16 [131072, 1152], P('dp'), may hold values from -6 to 6
- text_embed: bfloat16 [131072, 1152], P('dp'), may hold values from -6 to 6
- logit_scale: float32 [1], replicated, may hold values from 4 to 16
- logit_bias: float32 [1], replicated, may hold values from -4 to -1
Outputs:
- grad_images: float32 [131072, 1152], P('dp')
- grad_texts: float32 [131072, 1152], P('dp')
The draws below stay inside these ranges and needn't reach their ends.
All inputs are finite; a program needn't handle non-finite values.
Results may differ from the reference program's by a relative error of at most 0.005.
Values may be sent and summed in bfloat16 or wider, within the bound.
A program may use at most 128 MiB of HBM per device.

```python
import math
import jax
import jax.numpy as jnp
from jax import lax

D = 1152
B_DEV = 1024
CYCLE = 2
BATCH = 131072


def level_of(own_key, extent, split, least, high):
    def one(dim, blocks):
        draws = jax.random.uniform(jax.random.fold_in(jax.random.fold_in(own_key, 6), dim), (blocks,), jnp.float32, least / len(split), high / len(split))
        return jnp.repeat(jnp.exp(draws), extent[dim] // blocks).reshape((-1,) + (1,) * (len(extent) - dim - 1))

    gain = one(*split[0])
    for cut in split[1:]:
        gain = gain * one(*cut)
    return gain


def normal_values(stream_key, extent, width, reach, split=(), kind=jnp.bfloat16):
    result = width * jax.random.normal(stream_key, extent, jnp.float32)
    if split:
        result = result * level_of(stream_key, extent, split, -0.22, 0.18)
    return jnp.clip(result, -reach, reach).astype(kind)


def setup_inputs(seed: int = 0) -> dict:
    splits = jax.random.split(jax.random.key(seed), 5)
    image_embed = normal_values(splits[0], (BATCH, D), 1.0, 6.0, ((0, 128),))
    text_embed = normal_values(splits[1], (BATCH, D), 1.0, 6.0, ((0, 128),))
    logit_scale = jnp.clip(jnp.exp(jax.random.uniform(splits[2], (1,), jnp.float32, math.log(4.0), math.log(16.0))), 4.0, 16.0)
    logit_bias = jnp.clip(jax.random.uniform(splits[3], (1,), jnp.float32, -4.0, -1.0), -4.0, -1.0)
    return {"image_embed": image_embed, "text_embed": text_embed, "logit_scale": logit_scale, "logit_bias": logit_bias}


def normalize(raw):
    values = raw.astype(jnp.float32)
    scale_row = lax.rsqrt(lax.optimization_barrier(jnp.sum(values * values, axis=1, keepdims=True)) + 1e-06)
    return (values * scale_row, scale_row)

def reference(image_embed, text_embed, logit_scale, logit_bias):
    temper = logit_scale[0]
    offset = logit_bias[0]
    ximg, rx = normalize(image_embed)
    ytxt, ry = normalize(text_embed)
    ximg_b = ximg.astype(jnp.bfloat16)
    ytxt_b = ytxt.astype(jnp.bfloat16)
    blocks = BATCH // B_DEV
    xs = ximg_b.reshape(blocks, B_DEV, D)
    eye_mask = jnp.eye(B_DEV, dtype=jnp.float32)
    grad_x = jnp.zeros((blocks, B_DEV, D), jnp.float32)
    grad_y = jnp.zeros((BATCH, D), jnp.float32)
    for step in range(CYCLE + 1):
        shifted = jnp.roll(ytxt_b, step * B_DEV, axis=0).reshape(blocks, B_DEV, D)
        positive = eye_mask if step == 0 else jnp.zeros_like(eye_mask)

        def one_block(pair):
            xblock, yblock = pair
            logits = temper * jnp.dot(xblock, yblock.T, preferred_element_type=jnp.float32) + offset
            coef = (temper * (jax.nn.sigmoid(logits) - positive)).astype(jnp.bfloat16)
            gx_term = jnp.dot(coef, yblock, preferred_element_type=jnp.float32)
            gy_term = jnp.dot(coef.T, xblock, preferred_element_type=jnp.float32)
            return (gx_term, gy_term)
        gx_terms, gy_terms = lax.map(one_block, (xs, shifted))
        grad_x = grad_x + gx_terms
        grad_y = grad_y + jnp.roll(gy_terms.reshape(BATCH, D), -step * B_DEV, axis=0)
    grad_x = grad_x.reshape(BATCH, D)
    grad_images = (grad_x - ximg * lax.optimization_barrier(jnp.sum(ximg * grad_x, axis=1, keepdims=True))) * rx
    grad_texts = (grad_y - ytxt * lax.optimization_barrier(jnp.sum(ytxt * grad_y, axis=1, keepdims=True))) * ry
    return (grad_images, grad_texts)
```

```python
import functools

import jax
import jax.numpy as jnp
from jax import lax
from jax.experimental import pallas as pl
from jax.experimental.pallas import tpu as pltpu
from jax.sharding import PartitionSpec as P

MESH = pl.DeviceIdType.MESH
CHUNKS = 4
PIECES = 16
STRIPS = 2
IMG, TXT = 0, 1


def unit_rows(raw):
    values = raw.astype(jnp.float32)
    scale_row = lax.rsqrt(jnp.sum(values * values, axis=1, keepdims=True) + 1e-06)
    return values * scale_row, scale_row


def kernel(
    n,
    scale_ref,
    bias_ref,
    image_ref,
    text_ref,
    grad,
    raw,
    unit,
    far,
    cross,
    moving,
    terms,
    far_terms,
    cross_out,
    cross_in,
    far_out,
    far_in,
    load_sem,
    far_send,
    far_recv,
    cross_send,
    cross_recv,
    cross_out_send,
    cross_in_recv,
    far_out_send,
    far_in_recv,
):
    me = lax.axis_index("dp")
    odd = lax.rem(me, 2)
    up = lax.rem(me + n + 4 * odd - 2, n)
    down = lax.rem(me + n + 2 - 4 * odd, n)
    partner = me + 1 - 2 * odd
    still, sent = 1 - odd, odd
    rows = image_ref.shape[0]
    chunk = rows // CHUNKS
    piece = rows // PIECES
    strip = rows // STRIPS
    temper = scale_ref[0]
    offset = bias_ref[0]

    def load(which, ref):
        return pltpu.make_async_copy(ref, raw.at[which], load_sem.at[which])

    def to_up(source, j):
        at = pl.ds(j * chunk, chunk)
        return pltpu.make_async_remote_copy(
            source.at[at], far.at[at], far_send.at[j], far_recv.at[j], device_id=(up,), device_id_type=MESH
        )

    def to_partner(source, j):
        at = pl.ds(j * chunk, chunk)
        return pltpu.make_async_remote_copy(
            source.at[at], cross.at[at], cross_send.at[j], cross_recv.at[j], device_id=(partner,), device_id_type=MESH
        )

    def terms_to_partner(j):
        at = pl.ds(j * chunk, chunk)
        return pltpu.make_async_remote_copy(
            cross_out.at[at],
            cross_in.at[at],
            cross_out_send.at[j],
            cross_in_recv.at[j],
            device_id=(partner,),
            device_id_type=MESH,
        )

    def terms_to_down(k):
        at = pl.ds(k * piece, piece)
        return pltpu.make_async_remote_copy(
            far_out.at[at], far_in.at[at], far_out_send.at[k], far_in_recv.at[k], device_id=(down,), device_id_type=MESH
        )

    load(IMG, image_ref).start()
    load(TXT, text_ref).start()
    barrier = pltpu.get_barrier_semaphore()
    for other in (up, down, partner):
        pl.semaphore_signal(barrier, inc=1, device_id=(other,), device_id_type=MESH)
    pl.semaphore_wait(barrier, 3)

    @pl.when(odd == 1)
    def _():
        for j in range(CHUNKS):
            to_up(text_ref, j).start()

    @pl.when(odd == 0)
    def _():
        for j in range(CHUNKS):
            to_up(image_ref, j).start()
        for j in range(CHUNKS):
            to_partner(text_ref, j).start()

    grad[...] = jnp.zeros_like(grad)
    load(IMG, image_ref).wait()
    load(TXT, text_ref).wait()
    for which in (IMG, TXT):

        @pl.loop(0, PIECES)
        def _(k):
            at = pl.ds(k * piece, piece)
            unit[which, at] = unit_rows(raw[which, at])[0].astype(jnp.bfloat16)

    def interaction(which, held, out, diagonal=None):
        out[...] = jnp.zeros_like(out)

        @pl.loop(0, STRIPS)
        def _(i):
            at = pl.ds(i * strip, strip)
            x = unit[which, at]
            y = held[...]
            logits = (
                temper
                * lax.dot_general(x, y, (((1,), (1,)), ((), ())), preferred_element_type=jnp.float32)
                + offset
            )
            prob = jax.nn.sigmoid(logits)
            if diagonal is not None:
                row = lax.broadcasted_iota(jnp.int32, logits.shape, 0) + i * strip
                col = lax.broadcasted_iota(jnp.int32, logits.shape, 1) + diagonal * chunk
                prob = prob - jnp.where(row == col, 1.0, 0.0)
            coef = (temper * prob).astype(jnp.bfloat16)
            grad[which, at] += jnp.dot(coef, y, preferred_element_type=jnp.float32)
            out[...] += lax.dot_general(coef, x, (((0,), (0,)), ((), ())), preferred_element_type=jnp.float32)

    def own(j):
        at = pl.ds(j * chunk, chunk)
        interaction(IMG, unit.at[TXT, at], terms, diagonal=j)
        grad[TXT, at] += terms[...]

    def finish(j):
        at = pl.ds(j * chunk, chunk)
        terms_to_partner(j).wait_recv()

        @pl.when(odd == 1)
        def _():
            far_out[at] = (far_terms[at] + cross_in[at].astype(jnp.float32)).astype(jnp.bfloat16)

        @pl.when(odd == 0)
        def _():
            far_out[at] = far_terms[at].astype(jnp.bfloat16)
            grad[TXT, at] += cross_in[at].astype(jnp.float32)

    own(0)
    per = PIECES // CHUNKS

    @pl.loop(0, CHUNKS)
    def _(j):
        at = pl.ds(j * chunk, chunk)
        to_up(image_ref, j).wait_recv()

        @pl.when(odd == 1)
        def _():
            to_partner(far, j).start()

        @pl.when(j > 0)
        def _():
            finish(j - 1)

        @pl.when(j == CHUNKS - 1)
        def _():
            @pl.loop(0, per * (CHUNKS - 1))
            def _(k):
                terms_to_down(k).start()

        moving[...] = unit_rows(far[at])[0].astype(jnp.bfloat16)
        interaction(still, moving, far_terms.at[at])
        to_partner(text_ref, j).wait_recv()
        moving[...] = unit_rows(cross[at])[0].astype(jnp.bfloat16)
        interaction(IMG, moving, terms)
        cross_out[at] = terms[...].astype(jnp.bfloat16)
        terms_to_partner(j).start()

    finish(CHUNKS - 1)

    @pl.loop(per * (CHUNKS - 1), PIECES)
    def _(k):
        terms_to_down(k).start()

    @pl.loop(1, CHUNKS)
    def _(j):
        own(j)

    def project(which, at):
        values, scale_row = unit_rows(raw[which, at])
        total = grad[which, at]
        grad[which, at] = (total - values * jnp.sum(values * total, axis=1, keepdims=True)) * scale_row

    @pl.loop(0, PIECES)
    def _(k):
        project(still, pl.ds(k * piece, piece))

    @pl.loop(0, PIECES)
    def _(k):
        at = pl.ds(k * piece, piece)
        terms_to_down(k).wait_recv()
        grad[sent, at] += far_in[at].astype(jnp.float32)
        project(sent, at)

    for j in range(CHUNKS):
        to_up(image_ref, j).wait_send()
        to_partner(text_ref, j).wait_send()
        terms_to_partner(j).wait_send()
    for k in range(PIECES):
        terms_to_down(k).wait_send()


def on_device(n, image_embed, text_embed, logit_scale, logit_bias):
    rows, width = image_embed.shape
    chunk = rows // CHUNKS
    block = (rows, width)
    half = jnp.bfloat16
    dma = pltpu.SemaphoreType.DMA
    hbm = pl.BlockSpec(memory_space=pltpu.MemorySpace.HBM)
    smem = pl.BlockSpec(memory_space=pltpu.SMEM)
    grads = pl.pallas_call(
        functools.partial(kernel, n),
        out_shape=OUT((2, rows, width), jnp.float32),
        in_specs=[smem, smem, hbm, hbm],
        out_specs=pl.BlockSpec(memory_space=pltpu.VMEM),
        scratch_shapes=[
            pltpu.VMEM((2, rows, width), half),
            pltpu.VMEM((2, rows, width), half),
            pltpu.VMEM(block, half),
            pltpu.VMEM(block, half),
            pltpu.VMEM((chunk, width), half),
            pltpu.VMEM((chunk, width), jnp.float32),
            pltpu.VMEM(block, jnp.float32),
            pltpu.VMEM(block, half),
            pltpu.VMEM(block, half),
            pltpu.VMEM(block, half),
            pltpu.VMEM(block, half),
            dma((2,)),
            dma((CHUNKS,)),
            dma((CHUNKS,)),
            dma((CHUNKS,)),
            dma((CHUNKS,)),
            dma((CHUNKS,)),
            dma((CHUNKS,)),
            dma((PIECES,)),
            dma((PIECES,)),
        ],
        compiler_params=pltpu.CompilerParams(
            collective_id=0, has_side_effects=True, vmem_limit_bytes=VMEM_LIMIT
        ),
        cost_estimate=pl.CostEstimate(
            flops=18 * rows * rows * width, bytes_accessed=12 * rows * width, transcendentals=3 * rows * rows
        ),
    )(logit_scale, logit_bias, image_embed, text_embed)
    return grads[IMG], grads[TXT]


OUT = pltpu.MemorySpace.VMEM
VMEM_LIMIT = 44 * 1024 * 1024


def solution(mesh):
    placed = (P("dp", None), P("dp", None), P(), P())
    return jax.shard_map(
        functools.partial(on_device, mesh.shape["dp"]),
        mesh=mesh,
        in_specs=placed,
        out_specs=(P("dp", None), P("dp", None)),
        check_vma=False,
    )
```

```python
import functools

import jax
import jax.numpy as jnp
from jax import lax
from jax.experimental import pallas as pl
from jax.experimental.pallas import tpu as pltpu
from jax.sharding import PartitionSpec as P

MESH = pl.DeviceIdType.MESH
CHUNKS = 4
PIECES = 16
PARTS = 8
OWN_FIRST = 2
WRITES = 4
STRIPS = 2
IMG, TXT = 0, 1
BEFORE_FAR = {2: ((0, 0),), 3: ((1, 1), (0, 2))}
AFTER_FAR = {2: ((1, 0), (0, 1)), 3: ((1, 2), (0, 3))}


def unit_rows(raw):
    values = raw.astype(jnp.float32)
    scale_row = lax.rsqrt(jnp.sum(values * values, axis=1, keepdims=True) + 1e-06)
    return values * scale_row, scale_row


def kernel(
    n,
    scale_ref,
    bias_ref,
    image_ref,
    text_ref,
    grad,
    raw,
    unit,
    far,
    cross,
    far_unit,
    terms,
    far_terms,
    cross_out,
    cross_in,
    far_out,
    far_in,
    load_sem,
    far_send,
    far_recv,
    cross_send,
    cross_recv,
    cross_out_send,
    cross_in_recv,
    far_out_send,
    far_in_recv,
):
    me = lax.axis_index("dp")
    odd = lax.rem(me, 2)
    up = lax.rem(me + n + 4 * odd - 2, n)
    down = lax.rem(me + n + 2 - 4 * odd, n)
    partner = me + 1 - 2 * odd
    still, sent = 1 - odd, odd
    rows = image_ref.shape[0]
    chunk = rows // CHUNKS
    piece = rows // PIECES
    part = rows // PARTS
    strip = rows // STRIPS

    def load(which, ref):
        return pltpu.make_async_copy(ref, raw.at[which], load_sem.at[which])

    def to_up(source, k):
        at = pl.ds(k * part, part)
        return pltpu.make_async_remote_copy(
            source.at[at], far.at[at], far_send.at[k], far_recv.at[k], device_id=(up,), device_id_type=MESH
        )

    def to_partner(source, k):
        at = pl.ds(k * part, part)
        return pltpu.make_async_remote_copy(
            source.at[at], cross.at[at], cross_send.at[k], cross_recv.at[k], device_id=(partner,), device_id_type=MESH
        )

    def terms_to_partner(j):
        at = pl.ds(j * chunk, chunk)
        return pltpu.make_async_remote_copy(
            cross_out.at[at],
            cross_in.at[at],
            cross_out_send.at[j],
            cross_in_recv.at[j],
            device_id=(partner,),
            device_id_type=MESH,
        )

    def terms_to_down(k):
        at = pl.ds(k * piece, piece)
        return pltpu.make_async_remote_copy(
            far_out.at[at], far_in.at[at], far_out_send.at[k], far_in_recv.at[k], device_id=(down,), device_id_type=MESH
        )

    load(IMG, image_ref).start()
    load(TXT, text_ref).start()
    barrier = pltpu.get_barrier_semaphore()
    for other in (up, down, partner):
        pl.semaphore_signal(barrier, inc=1, device_id=(other,), device_id_type=MESH)
    pl.semaphore_wait(barrier, 3)

    @pl.when(odd == 1)
    def _():
        for k in range(PARTS):
            to_up(text_ref, k).start()

    @pl.when(odd == 0)
    def _():
        for k in range(PARTS):
            to_up(image_ref, k).start()

    load(TXT, text_ref).wait()
    load(IMG, image_ref).wait()
    for which in (TXT, IMG):

        @pl.loop(0, PARTS)
        def _(k):
            at = pl.ds(k * part, part)
            unit[which, at] = unit_rows(raw[which, at])[0].astype(jnp.bfloat16)

        if which == TXT:

            @pl.when(odd == 0)
            def _():
                for k in range(PARTS):
                    to_partner(unit.at[TXT], k).start()

    temper = scale_ref[0]
    offset = bias_ref[0]

    def interaction(which, held, out, diagonal=None):
        y = held[...]

        def coefficients(i):
            x = unit[which, pl.ds(i * strip, strip)]
            logits = (
                temper
                * lax.dot_general(x, y, (((1,), (1,)), ((), ())), preferred_element_type=jnp.float32)
                + offset
            )
            prob = jax.nn.sigmoid(logits)
            if diagonal is not None:
                row = lax.broadcasted_iota(jnp.int32, logits.shape, 0) + i * strip
                col = lax.broadcasted_iota(jnp.int32, logits.shape, 1) + diagonal * chunk
                prob = prob - jnp.where(row == col, 1.0, 0.0)
            return x, (temper * prob).astype(jnp.bfloat16)

        ahead = coefficients(0)
        for i in range(STRIPS):
            at = pl.ds(i * strip, strip)
            x, coef = ahead
            if i < STRIPS - 1:
                ahead = coefficients(i + 1)
            mine = jnp.dot(coef, y, preferred_element_type=jnp.float32)
            theirs = lax.dot_general(coef, x, (((0,), (0,)), ((), ())), preferred_element_type=jnp.float32)
            if diagonal == 0:
                grad[which, at] = mine
            else:
                grad[which, at] += mine
            if i == 0:
                terms[...] = theirs
            elif i < STRIPS - 1:
                terms[...] += theirs
            elif diagonal is not None and diagonal >= OWN_FIRST:
                out[...] += terms[...] + theirs
            else:
                out[...] = (terms[...] + theirs).astype(out.dtype)

    per = PIECES // CHUNKS
    per_part = PARTS // CHUNKS

    def give_back(j, parity):
        @pl.when(odd == parity)
        def _():
            if parity == 1:
                terms_to_partner(j).wait_recv()
            for k in range(j * per, (j + 1) * per):
                at = pl.ds(k * piece, piece)
                total = far_terms[at]
                if parity == 1:
                    total = total + cross_in[at].astype(jnp.float32)
                far_out[at] = total.astype(jnp.bfloat16)
                terms_to_down(k).start()

    def own(j):
        at = pl.ds(j * chunk, chunk)
        interaction(IMG, unit.at[TXT, at], grad.at[TXT, at], diagonal=j)

    rest = pl.ds(OWN_FIRST * chunk, rows - OWN_FIRST * chunk)
    grad[TXT, rest] = jnp.zeros_like(grad[TXT, rest])
    for j in range(OWN_FIRST):
        own(j)

    for j in range(CHUNKS):
        at = pl.ds(j * chunk, chunk)
        for parity, earlier in BEFORE_FAR.get(j, ()):
            give_back(earlier, parity)

        @pl.loop(j * per_part, (j + 1) * per_part)
        def _(k):
            to_up(image_ref, k).wait_recv()
            here = pl.ds(k * part, part)
            far_unit[here] = unit_rows(far[here])[0].astype(jnp.bfloat16)

            @pl.when(odd == 1)
            def _():
                to_partner(far_unit, k).start()

        interaction(still, far_unit.at[at], far_terms.at[at])
        for parity, earlier in AFTER_FAR.get(j, ()):
            give_back(earlier, parity)

        @pl.loop(j * per_part, (j + 1) * per_part)
        def _(k):
            to_partner(far_unit, k).wait_recv()

        interaction(IMG, cross.at[at], cross_out.at[at])
        terms_to_partner(j).start()

    give_back(CHUNKS - 1, 1)
    for j in range(OWN_FIRST, CHUNKS):
        own(j)

    @pl.when(odd == 0)
    def _():
        @pl.loop(0, CHUNKS)
        def _(j):
            at = pl.ds(j * chunk, chunk)
            terms_to_partner(j).wait_recv()
            grad[TXT, at] += cross_in[at].astype(jnp.float32)

    def project(which, at):
        values, scale_row = unit_rows(raw[which, at])
        total = grad[which, at]
        grad[which, at] = (total - values * jnp.sum(values * total, axis=1, keepdims=True)) * scale_row

    @pl.loop(0, PIECES)
    def _(k):
        project(still, pl.ds(k * piece, piece))

    def back(k):
        at = pl.ds(k * piece, piece)
        terms_to_down(k).wait_recv()
        grad[sent, at] += far_in[at].astype(jnp.float32)
        project(sent, at)

    for j in range(CHUNKS):
        @pl.loop(j * per, (j + 1) * per)
        def _(k):
            back(k)

    for k in range(PARTS):
        to_up(image_ref, k).wait_send()
        to_partner(far_unit, k).wait_send()
    for j in range(CHUNKS):
        terms_to_partner(j).wait_send()
    for k in range(PIECES):
        terms_to_down(k).wait_send()


def write(both, image_grad, text_grad, sem):
    piece = both.shape[1] // WRITES

    def copy(which, k):
        at = pl.ds(k * piece, piece)
        return pltpu.make_async_copy(
            both.at[which, at], (image_grad, text_grad)[which].at[at], sem.at[which, k]
        )

    for k in range(WRITES):
        for which in (IMG, TXT):
            copy(which, k).start()
    for k in range(WRITES):
        for which in (IMG, TXT):
            copy(which, k).wait()


def on_device(n, image_embed, text_embed, logit_scale, logit_bias):
    rows, width = image_embed.shape
    chunk = rows // CHUNKS
    block = (rows, width)
    half = jnp.bfloat16
    dma = pltpu.SemaphoreType.DMA
    hbm = pl.BlockSpec(memory_space=pltpu.MemorySpace.HBM)
    smem = pl.BlockSpec(memory_space=pltpu.SMEM)
    grads = pl.pallas_call(
        functools.partial(kernel, n),
        out_shape=OUT((2, rows, width), jnp.float32),
        in_specs=[smem, smem, hbm, hbm],
        out_specs=pl.BlockSpec(memory_space=pltpu.VMEM),
        scratch_shapes=[
            pltpu.VMEM((2, rows, width), half),
            pltpu.VMEM((2, rows, width), half),
            pltpu.VMEM(block, half),
            pltpu.VMEM(block, half),
            pltpu.VMEM(block, half),
            pltpu.VMEM((chunk, width), jnp.float32),
            pltpu.VMEM(block, jnp.float32),
            pltpu.VMEM(block, half),
            pltpu.VMEM(block, half),
            pltpu.VMEM(block, half),
            pltpu.VMEM(block, half),
            dma((2,)),
            dma((PARTS,)),
            dma((PARTS,)),
            dma((PARTS,)),
            dma((PARTS,)),
            dma((CHUNKS,)),
            dma((CHUNKS,)),
            dma((PIECES,)),
            dma((PIECES,)),
        ],
        compiler_params=pltpu.CompilerParams(
            collective_id=0, has_side_effects=True, vmem_limit_bytes=VMEM_LIMIT
        ),
        cost_estimate=pl.CostEstimate(
            flops=18 * rows * rows * width, bytes_accessed=12 * rows * width, transcendentals=3 * rows * rows
        ),
    )(logit_scale, logit_bias, image_embed, text_embed)
    result = jax.ShapeDtypeStruct(block, jnp.float32)
    return pl.pallas_call(
        write,
        out_shape=(result, result),
        in_specs=[pl.BlockSpec(memory_space=pl.ANY)],
        out_specs=(hbm, hbm),
        compiler_params=pltpu.CompilerParams(vmem_limit_bytes=2 * 1024 * 1024),
        scratch_shapes=[dma((2, WRITES))],
        cost_estimate=pl.CostEstimate(flops=0, bytes_accessed=8 * rows * width, transcendentals=0),
    )(grads)


OUT = pltpu.MemorySpace.VMEM
VMEM_LIMIT = 50 * 1024 * 1024


def solution(mesh):
    placed = (P("dp", None), P("dp", None), P(), P())
    return jax.shard_map(
        functools.partial(on_device, mesh.shape["dp"]),
        mesh=mesh,
        in_specs=placed,
        out_specs=(P("dp", None), P("dp", None)),
        check_vma=False,
    )
```

```python
import functools

import jax
import jax.numpy as jnp
from jax import lax
from jax.experimental import pallas as pl
from jax.experimental.pallas import tpu as pltpu
from jax.sharding import PartitionSpec as P

MESH = pl.DeviceIdType.MESH
CHUNKS = 4
PIECES = 16
PARTS = 8
OWN_FIRST = 2
WRITES = 4
STRIPS = 2
IMG, TXT = 0, 1
BEFORE_FAR = {2: ((0, 2, 4),), 3: ((1, 4, 8), (0, 8, 12))}
AFTER_FAR = {1: ((0, 0, 2),), 2: ((1, 0, 4), (0, 4, 8)), 3: ((1, 8, 12), (0, 12, 16))}


def unit_rows(raw):
    values = raw.astype(jnp.float32)
    scale_row = lax.rsqrt(jnp.sum(values * values, axis=1, keepdims=True) + 1e-06)
    return values * scale_row, scale_row


def kernel(
    n,
    scale_ref,
    bias_ref,
    image_ref,
    text_ref,
    grad,
    raw,
    unit,
    far,
    cross,
    far_unit,
    scalars,
    terms,
    far_terms,
    cross_out,
    cross_in,
    far_out,
    far_in,
    from_down,
    from_partner,
    load_sem,
    scalar_sem,
    far_send,
    far_recv,
    cross_send,
    cross_recv,
    cross_out_send,
    cross_in_recv,
    far_out_send,
    far_in_recv,
):
    me = lax.axis_index("dp")
    odd = lax.rem(me, 2)
    up = lax.rem(me + n + 4 * odd - 2, n)
    down = lax.rem(me + n + 2 - 4 * odd, n)
    partner = me + 1 - 2 * odd
    still, sent = 1 - odd, odd
    rows = image_ref.shape[0]
    chunk = rows // CHUNKS
    piece = rows // PIECES
    part = rows // PARTS
    strip = rows // STRIPS

    def load(which, ref):
        return pltpu.make_async_copy(ref, raw.at[which], load_sem.at[which])

    def load_scalar(which, ref):
        return pltpu.make_async_copy(ref, scalars.at[which], scalar_sem.at[which])

    def to_up(source, k):
        at = pl.ds(k * part, part)
        return pltpu.make_async_remote_copy(
            source.at[at], far.at[at], far_send.at[k], far_recv.at[k], device_id=(up,), device_id_type=MESH
        )

    def to_partner(source, k):
        at = pl.ds(k * part, part)
        return pltpu.make_async_remote_copy(
            source.at[at], cross.at[at], cross_send.at[k], cross_recv.at[k], device_id=(partner,), device_id_type=MESH
        )

    def terms_to_partner(j):
        at = pl.ds(j * chunk, chunk)
        return pltpu.make_async_remote_copy(
            cross_out.at[at],
            cross_in.at[at],
            cross_out_send.at[j],
            cross_in_recv.at[j],
            device_id=(partner,),
            device_id_type=MESH,
        )

    def terms_to_down(k):
        at = pl.ds(k * piece, piece)
        return pltpu.make_async_remote_copy(
            far_out.at[at], far_in.at[at], far_out_send.at[k], far_in_recv.at[k], device_id=(down,), device_id_type=MESH
        )

    load(IMG, image_ref).start()
    load(TXT, text_ref).start()
    load_scalar(0, scale_ref).start()
    load_scalar(1, bias_ref).start()
    barrier = pltpu.get_barrier_semaphore()
    pl.semaphore_signal(barrier, inc=1, device_id=(down,), device_id_type=MESH)

    @pl.when(odd == 1)
    def _():
        pl.semaphore_signal(barrier, inc=1, device_id=(partner,), device_id_type=MESH)

    pl.semaphore_wait(barrier, 2 - odd)

    @pl.when(odd == 1)
    def _():
        for k in range(PARTS):
            to_up(text_ref, k).start()

    @pl.when(odd == 0)
    def _():
        for k in range(PARTS):
            to_up(image_ref, k).start()
        pl.semaphore_signal(from_partner, inc=1, device_id=(partner,), device_id_type=MESH)

    pl.semaphore_signal(from_down, inc=1, device_id=(up,), device_id_type=MESH)

    load(TXT, text_ref).wait()
    load(IMG, image_ref).wait()
    for which in (TXT, IMG):

        @pl.loop(0, PARTS)
        def _(k):
            at = pl.ds(k * part, part)
            unit[which, at] = unit_rows(raw[which, at])[0].astype(jnp.bfloat16)

        if which == TXT:

            @pl.when(odd == 0)
            def _():
                for k in range(PARTS):
                    to_partner(unit.at[TXT], k).start()

    load_scalar(0, scale_ref).wait()
    load_scalar(1, bias_ref).wait()
    temper = scalars[0, 0, 0]
    offset = scalars[1, 0, 0]

    def interaction(which, held, out, diagonal=None):
        y = held[...]

        def coefficients(i):
            x = unit[which, pl.ds(i * strip, strip)]
            logits = (
                temper
                * lax.dot_general(x, y, (((1,), (1,)), ((), ())), preferred_element_type=jnp.float32)
                + offset
            )
            prob = jax.nn.sigmoid(logits)
            if diagonal is not None:
                row = lax.broadcasted_iota(jnp.int32, logits.shape, 0) + i * strip
                col = lax.broadcasted_iota(jnp.int32, logits.shape, 1) + diagonal * chunk
                prob = prob - jnp.where(row == col, 1.0, 0.0)
            return x, (temper * prob).astype(jnp.bfloat16)

        ahead = coefficients(0)
        for i in range(STRIPS):
            at = pl.ds(i * strip, strip)
            x, coef = ahead
            if i < STRIPS - 1:
                ahead = coefficients(i + 1)
            mine = jnp.dot(coef, y, preferred_element_type=jnp.float32)
            theirs = lax.dot_general(coef, x, (((0,), (0,)), ((), ())), preferred_element_type=jnp.float32)
            if diagonal == 0:
                grad[which, at] = mine
            else:
                grad[which, at] += mine
            if i == 0:
                terms[...] = theirs
            elif i < STRIPS - 1:
                terms[...] += theirs
            elif diagonal is not None and diagonal >= OWN_FIRST:
                out[...] += terms[...] + theirs
            else:
                out[...] = (terms[...] + theirs).astype(out.dtype)

    per = PIECES // CHUNKS
    per_part = PARTS // CHUNKS

    def give_back(parity, first, last):
        @pl.when(odd == parity)
        def _():
            for k in range(first, last):
                if parity == 1 and k % per == 0:
                    terms_to_partner(k // per).wait_recv()
                at = pl.ds(k * piece, piece)
                total = far_terms[at]
                if parity == 1:
                    total = total + cross_in[at].astype(jnp.float32)
                far_out[at] = total.astype(jnp.bfloat16)
                terms_to_down(k).start()

    def own(j):
        at = pl.ds(j * chunk, chunk)
        interaction(IMG, unit.at[TXT, at], grad.at[TXT, at], diagonal=j)

    rest = pl.ds(OWN_FIRST * chunk, rows - OWN_FIRST * chunk)
    grad[TXT, rest] = jnp.zeros_like(grad[TXT, rest])
    for j in range(OWN_FIRST):
        own(j)

    pl.semaphore_wait(from_down, 1)

    @pl.when(odd == 1)
    def _():
        pl.semaphore_wait(from_partner, 1)

    for j in range(CHUNKS):
        at = pl.ds(j * chunk, chunk)
        for pieces in BEFORE_FAR.get(j, ()):
            give_back(*pieces)

        @pl.loop(j * per_part, (j + 1) * per_part)
        def _(k):
            to_up(image_ref, k).wait_recv()
            here = pl.ds(k * part, part)
            far_unit[here] = unit_rows(far[here])[0].astype(jnp.bfloat16)

            @pl.when(odd == 1)
            def _():
                to_partner(far_unit, k).start()

        interaction(still, far_unit.at[at], far_terms.at[at])
        for pieces in AFTER_FAR.get(j, ()):
            give_back(*pieces)

        @pl.loop(j * per_part, (j + 1) * per_part)
        def _(k):
            to_partner(far_unit, k).wait_recv()

        interaction(IMG, cross.at[at], cross_out.at[at])
        terms_to_partner(j).start()

    give_back(1, PIECES - per, PIECES)
    for j in range(OWN_FIRST, CHUNKS):
        own(j)

    @pl.when(odd == 0)
    def _():
        @pl.loop(0, CHUNKS)
        def _(j):
            at = pl.ds(j * chunk, chunk)
            terms_to_partner(j).wait_recv()
            grad[TXT, at] += cross_in[at].astype(jnp.float32)

    def project(which, at):
        values, scale_row = unit_rows(raw[which, at])
        total = grad[which, at]
        grad[which, at] = (total - values * jnp.sum(values * total, axis=1, keepdims=True)) * scale_row

    @pl.loop(0, PIECES)
    def _(k):
        project(still, pl.ds(k * piece, piece))

    def back(k):
        at = pl.ds(k * piece, piece)
        terms_to_down(k).wait_recv()
        grad[sent, at] += far_in[at].astype(jnp.float32)
        project(sent, at)

    for j in range(CHUNKS):
        @pl.loop(j * per, (j + 1) * per)
        def _(k):
            back(k)

    for k in range(PARTS):
        to_up(image_ref, k).wait_send()
        to_partner(far_unit, k).wait_send()
    for j in range(CHUNKS):
        terms_to_partner(j).wait_send()
    for k in range(PIECES):
        terms_to_down(k).wait_send()


def write(both, image_grad, text_grad, sem):
    piece = both.shape[1] // WRITES

    def copy(which, k):
        at = pl.ds(k * piece, piece)
        return pltpu.make_async_copy(
            both.at[which, at], (image_grad, text_grad)[which].at[at], sem.at[which, k]
        )

    for k in range(WRITES):
        for which in (IMG, TXT):
            copy(which, k).start()
    for k in range(WRITES):
        for which in (IMG, TXT):
            copy(which, k).wait()


def on_device(n, image_embed, text_embed, logit_scale, logit_bias):
    rows, width = image_embed.shape
    chunk = rows // CHUNKS
    block = (rows, width)
    half = jnp.bfloat16
    dma = pltpu.SemaphoreType.DMA
    hbm = pl.BlockSpec(memory_space=pltpu.MemorySpace.HBM)
    grads = pl.pallas_call(
        functools.partial(kernel, n),
        out_shape=OUT((2, rows, width), jnp.float32),
        in_specs=[hbm] * 4,
        out_specs=pl.BlockSpec(memory_space=pltpu.VMEM),
        scratch_shapes=[
            pltpu.VMEM((2, rows, width), half),
            pltpu.VMEM((2, rows, width), half),
            pltpu.VMEM(block, half),
            pltpu.VMEM(block, half),
            pltpu.VMEM(block, half),
            pltpu.SMEM((2, 1, 1), jnp.float32),
            pltpu.VMEM((chunk, width), jnp.float32),
            pltpu.VMEM(block, jnp.float32),
            pltpu.VMEM(block, half),
            pltpu.VMEM(block, half),
            pltpu.VMEM(block, half),
            pltpu.VMEM(block, half),
            pltpu.SemaphoreType.REGULAR,
            pltpu.SemaphoreType.REGULAR,
            dma((2,)),
            dma((2,)),
            dma((PARTS,)),
            dma((PARTS,)),
            dma((PARTS,)),
            dma((PARTS,)),
            dma((CHUNKS,)),
            dma((CHUNKS,)),
            dma((PIECES,)),
            dma((PIECES,)),
        ],
        compiler_params=pltpu.CompilerParams(
            collective_id=0, has_side_effects=True, vmem_limit_bytes=VMEM_LIMIT
        ),
        cost_estimate=pl.CostEstimate(
            flops=18 * rows * rows * width, bytes_accessed=12 * rows * width, transcendentals=3 * rows * rows
        ),
    )(logit_scale.reshape(1, 1), logit_bias.reshape(1, 1), image_embed, text_embed)
    result = jax.ShapeDtypeStruct(block, jnp.float32)
    return pl.pallas_call(
        write,
        out_shape=(result, result),
        in_specs=[pl.BlockSpec(memory_space=pl.ANY)],
        out_specs=(hbm, hbm),
        compiler_params=pltpu.CompilerParams(vmem_limit_bytes=2 * 1024 * 1024),
        scratch_shapes=[dma((2, WRITES))],
        cost_estimate=pl.CostEstimate(flops=0, bytes_accessed=8 * rows * width, transcendentals=0),
    )(grads)


OUT = pltpu.MemorySpace.VMEM
VMEM_LIMIT = 50 * 1024 * 1024


def solution(mesh):
    placed = (P("dp", None), P("dp", None), P(), P())
    return jax.shard_map(
        functools.partial(on_device, mesh.shape["dp"]),
        mesh=mesh,
        in_specs=placed,
        out_specs=(P("dp", None), P("dp", None)),
        check_vma=False,
    )
```

```python
import functools

import jax
import jax.numpy as jnp
from jax import lax
from jax.experimental import pallas as pl
from jax.experimental.pallas import tpu as pltpu
from jax.sharding import PartitionSpec as P

MESH = pl.DeviceIdType.MESH
CHUNKS = 4
PIECES = 16
PARTS = 8
OWN_FIRST = 2
WRITES = 4
STRIPS = 2
IMG, TXT = 0, 1
BEFORE_FAR = {2: ((0, 2, 4),), 3: ((1, 4, 8), (0, 8, 12))}
AFTER_FAR = {1: ((0, 0, 2),), 2: ((1, 0, 4), (0, 4, 8)), 3: ((1, 8, 12), (0, 12, 16))}


def unit_rows(raw):
    values = raw.astype(jnp.float32)
    scale_row = lax.rsqrt(jnp.sum(values * values, axis=1, keepdims=True) + 1e-06)
    return values * scale_row, scale_row


def kernel(
    n,
    scale_ref,
    bias_ref,
    image_ref,
    text_ref,
    grad,
    raw,
    unit,
    far,
    cross,
    far_unit,
    terms,
    far_terms,
    cross_out,
    cross_in,
    far_out,
    far_in,
    from_down,
    from_partner,
    load_sem,
    far_send,
    far_recv,
    cross_send,
    cross_recv,
    cross_out_send,
    cross_in_recv,
    far_out_send,
    far_in_recv,
):
    me = lax.axis_index("dp")
    odd = lax.rem(me, 2)
    up = lax.rem(me + n + 4 * odd - 2, n)
    down = lax.rem(me + n + 2 - 4 * odd, n)
    partner = me + 1 - 2 * odd
    still, sent = 1 - odd, odd
    rows = image_ref.shape[0]
    chunk = rows // CHUNKS
    piece = rows // PIECES
    part = rows // PARTS
    strip = rows // STRIPS

    def load(which, ref):
        return pltpu.make_async_copy(ref, raw.at[which], load_sem.at[which])

    def to_up(source, k):
        at = pl.ds(k * part, part)
        return pltpu.make_async_remote_copy(
            source.at[at], far.at[at], far_send.at[k], far_recv.at[k], device_id=(up,), device_id_type=MESH
        )

    def to_partner(source, k):
        at = pl.ds(k * part, part)
        return pltpu.make_async_remote_copy(
            source.at[at], cross.at[at], cross_send.at[k], cross_recv.at[k], device_id=(partner,), device_id_type=MESH
        )

    def terms_to_partner(j):
        at = pl.ds(j * chunk, chunk)
        return pltpu.make_async_remote_copy(
            cross_out.at[at],
            cross_in.at[at],
            cross_out_send.at[j],
            cross_in_recv.at[j],
            device_id=(partner,),
            device_id_type=MESH,
        )

    def terms_to_down(k):
        at = pl.ds(k * piece, piece)
        return pltpu.make_async_remote_copy(
            far_out.at[at], far_in.at[at], far_out_send.at[k], far_in_recv.at[k], device_id=(down,), device_id_type=MESH
        )

    barrier = pltpu.get_barrier_semaphore()
    pl.semaphore_signal(barrier, inc=1, device_id=(down,), device_id_type=MESH)

    @pl.when(odd == 1)
    def _():
        pl.semaphore_signal(barrier, inc=1, device_id=(partner,), device_id_type=MESH)

    pl.semaphore_wait(barrier, 2 - odd)

    @pl.when(odd == 1)
    def _():
        for k in range(PARTS):
            to_up(text_ref, k).start()

    @pl.when(odd == 0)
    def _():
        for k in range(PARTS):
            to_up(image_ref, k).start()
        pl.semaphore_signal(from_partner, inc=1, device_id=(partner,), device_id_type=MESH)

    pl.semaphore_signal(from_down, inc=1, device_id=(up,), device_id_type=MESH)

    load(IMG, image_ref).start()
    load(TXT, text_ref).start()

    load(TXT, text_ref).wait()
    load(IMG, image_ref).wait()
    for which in (TXT, IMG):

        @pl.loop(0, PARTS)
        def _(k):
            at = pl.ds(k * part, part)
            unit[which, at] = unit_rows(raw[which, at])[0].astype(jnp.bfloat16)

        if which == TXT:

            @pl.when(odd == 0)
            def _():
                for k in range(PARTS):
                    to_partner(unit.at[TXT], k).start()

    temper = scale_ref[0]
    offset = bias_ref[0]

    def interaction(which, held, out, diagonal=None):
        y = held[...]

        def coefficients(i):
            x = unit[which, pl.ds(i * strip, strip)]
            logits = (
                temper
                * lax.dot_general(x, y, (((1,), (1,)), ((), ())), preferred_element_type=jnp.float32)
                + offset
            )
            prob = jax.nn.sigmoid(logits)
            if diagonal is not None:
                row = lax.broadcasted_iota(jnp.int32, logits.shape, 0) + i * strip
                col = lax.broadcasted_iota(jnp.int32, logits.shape, 1) + diagonal * chunk
                prob = prob - jnp.where(row == col, 1.0, 0.0)
            return x, (temper * prob).astype(jnp.bfloat16)

        ahead = coefficients(0)
        for i in range(STRIPS):
            at = pl.ds(i * strip, strip)
            x, coef = ahead
            if i < STRIPS - 1:
                ahead = coefficients(i + 1)
            mine = jnp.dot(coef, y, preferred_element_type=jnp.float32)
            theirs = lax.dot_general(coef, x, (((0,), (0,)), ((), ())), preferred_element_type=jnp.float32)
            if diagonal == 0:
                grad[which, at] = mine
            else:
                grad[which, at] += mine
            if i == 0:
                terms[...] = theirs
            elif i < STRIPS - 1:
                terms[...] += theirs
            elif diagonal is not None and diagonal >= OWN_FIRST:
                out[...] += terms[...] + theirs
            else:
                out[...] = (terms[...] + theirs).astype(out.dtype)

    per = PIECES // CHUNKS
    per_part = PARTS // CHUNKS

    def give_back(parity, first, last):
        @pl.when(odd == parity)
        def _():
            for k in range(first, last):
                if parity == 1 and k % per == 0:
                    terms_to_partner(k // per).wait_recv()
                at = pl.ds(k * piece, piece)
                total = far_terms[at]
                if parity == 1:
                    total = total + cross_in[at].astype(jnp.float32)
                far_out[at] = total.astype(jnp.bfloat16)
                terms_to_down(k).start()

    def own(j):
        at = pl.ds(j * chunk, chunk)
        interaction(IMG, unit.at[TXT, at], grad.at[TXT, at], diagonal=j)

    rest = pl.ds(OWN_FIRST * chunk, rows - OWN_FIRST * chunk)
    grad[TXT, rest] = jnp.zeros_like(grad[TXT, rest])
    for j in range(OWN_FIRST):
        own(j)

    pl.semaphore_wait(from_down, 1)

    @pl.when(odd == 1)
    def _():
        pl.semaphore_wait(from_partner, 1)

    for j in range(CHUNKS):
        at = pl.ds(j * chunk, chunk)
        for pieces in BEFORE_FAR.get(j, ()):
            give_back(*pieces)

        @pl.loop(j * per_part, (j + 1) * per_part)
        def _(k):
            to_up(image_ref, k).wait_recv()
            here = pl.ds(k * part, part)
            far_unit[here] = unit_rows(far[here])[0].astype(jnp.bfloat16)

            @pl.when(odd == 1)
            def _():
                to_partner(far_unit, k).start()

        interaction(still, far_unit.at[at], far_terms.at[at])
        for pieces in AFTER_FAR.get(j, ()):
            give_back(*pieces)

        @pl.loop(j * per_part, (j + 1) * per_part)
        def _(k):
            to_partner(far_unit, k).wait_recv()

        interaction(IMG, cross.at[at], cross_out.at[at])
        terms_to_partner(j).start()

    give_back(1, PIECES - per, PIECES)
    for j in range(OWN_FIRST, CHUNKS):
        own(j)

    @pl.when(odd == 0)
    def _():
        @pl.loop(0, CHUNKS)
        def _(j):
            at = pl.ds(j * chunk, chunk)
            terms_to_partner(j).wait_recv()
            grad[TXT, at] += cross_in[at].astype(jnp.float32)

    def project(which, at):
        values, scale_row = unit_rows(raw[which, at])
        total = grad[which, at]
        grad[which, at] = (total - values * jnp.sum(values * total, axis=1, keepdims=True)) * scale_row

    @pl.loop(0, PIECES)
    def _(k):
        project(still, pl.ds(k * piece, piece))

    for k in range(PARTS):
        to_up(image_ref, k).wait_send()
        to_partner(far_unit, k).wait_send()
    for j in range(CHUNKS):
        terms_to_partner(j).wait_send()

    @pl.loop(0, PIECES)
    def _(k):
        at = pl.ds(k * piece, piece)
        terms_to_down(k).wait_recv()
        grad[sent, at] += far_in[at].astype(jnp.float32)
        project(sent, at)
        terms_to_down(k).wait_send()


def write(both, image_grad, text_grad, sem):
    piece = both.shape[1] // WRITES

    def copy(which, k):
        at = pl.ds(k * piece, piece)
        return pltpu.make_async_copy(
            both.at[which, at], (image_grad, text_grad)[which].at[at], sem.at[which, k]
        )

    for k in range(WRITES):
        for which in (IMG, TXT):
            copy(which, k).start()
    for k in range(WRITES):
        for which in (IMG, TXT):
            copy(which, k).wait()


def on_device(n, image_embed, text_embed, logit_scale, logit_bias):
    rows, width = image_embed.shape
    chunk = rows // CHUNKS
    block = (rows, width)
    half = jnp.bfloat16
    dma = pltpu.SemaphoreType.DMA
    hbm = pl.BlockSpec(memory_space=pltpu.MemorySpace.HBM)
    smem = pl.BlockSpec(memory_space=pltpu.SMEM)
    grads = pl.pallas_call(
        functools.partial(kernel, n),
        out_shape=OUT((2, rows, width), jnp.float32),
        in_specs=[smem, smem, hbm, hbm],
        out_specs=pl.BlockSpec(memory_space=pltpu.VMEM),
        scratch_shapes=[
            pltpu.VMEM((2, rows, width), half),
            pltpu.VMEM((2, rows, width), half),
            pltpu.VMEM(block, half),
            pltpu.VMEM(block, half),
            pltpu.VMEM(block, half),
            pltpu.VMEM((chunk, width), jnp.float32),
            pltpu.VMEM(block, jnp.float32),
            pltpu.VMEM(block, half),
            pltpu.VMEM(block, half),
            pltpu.VMEM(block, half),
            pltpu.VMEM(block, half),
            pltpu.SemaphoreType.REGULAR,
            pltpu.SemaphoreType.REGULAR,
            dma((2,)),
            dma((PARTS,)),
            dma((PARTS,)),
            dma((PARTS,)),
            dma((PARTS,)),
            dma((CHUNKS,)),
            dma((CHUNKS,)),
            dma((PIECES,)),
            dma((PIECES,)),
        ],
        compiler_params=pltpu.CompilerParams(
            collective_id=0, has_side_effects=True, vmem_limit_bytes=VMEM_LIMIT
        ),
        cost_estimate=pl.CostEstimate(
            flops=18 * rows * rows * width, bytes_accessed=12 * rows * width, transcendentals=3 * rows * rows
        ),
    )(logit_scale, logit_bias, image_embed, text_embed)
    result = jax.ShapeDtypeStruct(block, jnp.float32)
    return pl.pallas_call(
        write,
        out_shape=(result, result),
        in_specs=[pl.BlockSpec(memory_space=pl.ANY)],
        out_specs=(hbm, hbm),
        compiler_params=pltpu.CompilerParams(vmem_limit_bytes=2 * 1024 * 1024),
        scratch_shapes=[dma((2, WRITES))],
        cost_estimate=pl.CostEstimate(flops=0, bytes_accessed=8 * rows * width, transcendentals=0),
    )(grads)


OUT = pltpu.MemorySpace.VMEM
VMEM_LIMIT = 50 * 1024 * 1024


def solution(mesh):
    placed = (P("dp", None), P("dp", None), P(), P())
    return jax.shard_map(
        functools.partial(on_device, mesh.shape["dp"]),
        mesh=mesh,
        in_specs=placed,
        out_specs=(P("dp", None), P("dp", None)),
        check_vma=False,
    )
```
